32 devices in a mesh: rows: 8 (over z, x), grp: 4 (over y, core).
Axes of the slice: x: 2, y: 2, z: 4, core: 2. Of those that a mesh axis runs over, the one named last changes fastest.
Arguments:
- embeddings: bfloat16 [131072, 1024], P(('rows', 'grp')), may hold values from -6 to 6
- residual: float32 [131072, 64], P(('rows', 'grp')), may hold values from -6 to 6
- block_ids: int32 [512], replicated, may hold values from 0 to 131071, as said below
Outputs:
- updated: float32 [131072, 64], P(('rows', 'grp'))
- change: float32 [512, 64], replicated
The draws below stay inside these ranges and needn't reach their ends.
Inputs may be any that keep to these rules, and one draw needn't show every extreme that they name: `block_ids`: 512 distinct row ids in increasing order; at most 32 of them lie in one device's 4096 consecutive rows, and some device holds exactly 32.
All inputs are finite; a program needn't handle non-finite values.
Results may differ from the reference program's by a relative error of at most 0.0065.
Values may be sent and summed in bfloat16 or wider, within the bound.
A program may use at most 64 MiB of HBM per device.

```python
import jax
import jax.numpy as jnp
from jax import lax

D = 1024
OUTS = 64
BLOCK = 512
ROWS_DEV = 4096
ROWS = 131072
N_ROWS = 8
N_GRP = 4


cluster_count = 64


def draw_embeddings(key, part):
    key = jax.random.fold_in(key, 5)
    subkeys = jax.random.split(key, 4)
    centres = jax.random.normal(subkeys[0], (cluster_count, D), jnp.float32)
    member = jax.random.randint(subkeys[1], (ROWS,), 0, cluster_count)
    jitter = jax.random.normal(subkeys[3], (ROWS, D), jnp.float32)
    values = 0.866 * centres[member] + 0.5 * jitter
    return jnp.clip(values, -6.0, 6.0).astype(jnp.bfloat16)


def draw_block_ids(key, part):
    key = jax.random.fold_in(key, 11)
    devices = N_ROWS * N_GRP
    capacity = max(2, 2 * BLOCK // devices)
    keys = jax.random.split(key, 4)
    weights = jax.random.randint(keys[0], (devices,), 0, 3)
    fullest = jax.random.randint(keys[1], (), 0, devices)
    weights = jnp.where(jnp.arange(devices) == fullest, 3, weights)
    noise = jax.random.randint(keys[2], (devices, capacity), 0, 1024)
    index = jnp.arange(devices * capacity).reshape(devices, capacity)
    score = (weights[:, None] * 1024 + noise) * (devices * capacity) + index
    _, picked = lax.top_k(score.reshape(-1), BLOCK)
    owners = picked // capacity
    slot_index = picked % capacity
    spacing = ROWS_DEV // capacity
    offsets = slot_index * spacing + jax.random.randint(keys[3], (BLOCK,), 0, spacing)
    return jnp.sort(owners * ROWS_DEV + offsets).astype(jnp.int32)


def level_of(stream_key, dims, cuts, least, top_value):
    factor_of, own = 1.0, jax.random.fold_in(stream_key, 6)
    for position, shards_of in cuts:
        steps = jnp.exp(jax.random.uniform(jax.random.fold_in(own, position), (shards_of,), jnp.float32, least / len(cuts), top_value / len(cuts)))
        factor_of = factor_of * jnp.repeat(steps, dims[position] // shards_of).reshape([-1 if axis == position else 1 for axis in range(len(dims))])
    return factor_of


def centred(key, extent, scale, most, cuts=(), held_as=jnp.bfloat16):
    result = scale * jax.random.normal(key, extent, jnp.float32)
    if cuts:
        result = result * level_of(key, extent, cuts, -0.22, 0.18)
    return jnp.clip(result, -most, most).astype(held_as)


def setup_inputs(seed: int = 0) -> dict:
    seeds = jax.random.split(jax.random.key(seed), 4)
    return {
        "embeddings": draw_embeddings(jax.random.fold_in(seeds[3], 71), 0),
        "residual": centred(seeds[1], (ROWS, OUTS), 1.0, 6.0, ((0, 32),), jnp.float32),
        "block_ids": draw_block_ids(jax.random.fold_in(seeds[3], 71), 0),
    }


ridge_weight = 0.5

def kernel_of(left, right, left_norms, right_norms, width):
    cross = jnp.dot(left.astype(jnp.float32), right.T.astype(jnp.float32), preferred_element_type=jnp.float32)
    dist = jnp.maximum(left_norms[:, None] + right_norms[None, :] - 2.0 * cross, 0.0)
    return jnp.exp(dist * (-2.0 / width))

def solve_block(factor, targets):
    inner = lax.linalg.triangular_solve(factor, targets, left_side=True, lower=True)
    return lax.linalg.triangular_solve(factor, inner, left_side=True, lower=True, transpose_a=True)

def reference(embeddings, residual, block_ids):
    width = embeddings.shape[1]
    block_emb = embeddings[block_ids]
    block_norms = jnp.sum(jnp.square(block_emb.astype(jnp.float32)), axis=1)
    block_kernel = kernel_of(block_emb, block_emb, block_norms, block_norms, width)
    block_kernel = block_kernel + ridge_weight * jnp.eye(block_kernel.shape[0], dtype=jnp.float32)
    block_res = residual[block_ids]
    factor = jnp.linalg.cholesky(block_kernel)
    change = solve_block(factor, block_res)
    change_bf = change.astype(jnp.bfloat16)
    shards = embeddings.reshape(-1, ROWS_DEV, width)
    res_shards = residual.reshape(-1, ROWS_DEV, residual.shape[1])

    def one_shard(pair):
        emb_rows, res_rows = pair
        row_norms = jnp.sum(jnp.square(emb_rows.astype(jnp.float32)), axis=1)
        columns = kernel_of(emb_rows, block_emb, row_norms, block_norms, width).astype(jnp.bfloat16)
        return res_rows - jnp.dot(columns.astype(jnp.float32), change_bf.astype(jnp.float32), preferred_element_type=jnp.float32)
    updated = lax.map(one_shard, (shards, res_shards)).reshape(residual.shape)
    updated = updated.at[block_ids].add(-ridge_weight * change)
    return (updated, change)
```

```python
import functools
import jax
import jax.numpy as jnp
from jax import lax
from jax.experimental import pallas as pl
from jax.experimental.pallas import tpu as pltpu
from jax.sharding import PartitionSpec as P

ridge_weight = 0.5
TILE = 128
STEP = 8
HIGH = lax.Precision.HIGHEST


def small_inverse(entries, n):
    a = {k: v for k, v in entries.items()}
    get = lambda i, j: a[(min(i, j), max(i, j))]
    for k in range(n):
        d = 1.0 / get(k, k)
        col = {i: get(i, k) for i in range(n) if i != k}
        scaled = {i: col[i] * d for i in col}
        for i in range(n):
            for j in range(i, n):
                if i != k and j != k:
                    a[(i, j)] = a[(i, j)] - scaled[i] * col[j]
        for i in col:
            a[(min(i, k), max(i, k))] = scaled[i]
        a[(k, k)] = -d
    return {k: -v for k, v in a.items()}


def tile_inverse(m):
    lane = lax.broadcasted_iota(jnp.int32, (8, TILE), 1)
    sub = lax.broadcasted_iota(jnp.int32, (8, TILE), 0)
    m = list(m)
    groups = TILE // 8
    for p in range(groups):
        c0 = p * STEP
        panel = m[p]
        entries = {
            (i, j): jnp.broadcast_to(panel[i:i + 1, c0 + j:c0 + j + 1], (8, TILE))
            for i in range(STEP) for j in range(i, STEP)
        }
        inv = small_inverse(entries, STEP)
        inside = (lane >= c0) & (lane < c0 + STEP)
        unit = jnp.where(lane - c0 == sub, 1.0, 0.0)
        augmented = jnp.where(inside, unit, panel)
        rows = [jnp.broadcast_to(augmented[j:j + 1, :], (8, TILE)) for j in range(STEP)]
        new_rows = []
        for i in range(STEP):
            acc = None
            for j in range(STEP):
                term = inv[(min(i, j), max(i, j))] * rows[j]
                acc = term if acc is None else acc + term
            new_rows.append(acc)
        for v in range(groups):
            if v == p:
                continue
            acc = jnp.where(inside, 0.0, m[v])
            for j in range(STEP):
                coef = jnp.broadcast_to(m[v][:, c0 + j:c0 + j + 1], (8, TILE))
                acc = acc - coef * new_rows[j]
            m[v] = acc
        acc = new_rows[0]
        for j in range(1, STEP):
            acc = jnp.where(sub == j, new_rows[j], acc)
        m[p] = acc
    return m


def dot(a, b, dims=((1,), (0,))):
    return lax.dot_general(a, b, (dims, ((), ())), precision=HIGH, preferred_element_type=jnp.float32)


def gram_kernel(cross, width):
    n = cross.shape[0]
    eye = (lax.broadcasted_iota(jnp.int32, (n, n), 0) == lax.broadcasted_iota(jnp.int32, (n, n), 1))
    diag = jnp.where(eye, cross, 0.0)
    row_norms = jnp.sum(diag, axis=0, keepdims=True)
    col_norms = jnp.sum(diag, axis=1, keepdims=True)
    dist = jnp.maximum(col_norms + row_norms - 2.0 * cross, 0.0)
    return jnp.exp(dist * (-2.0 / width)) + jnp.where(eye, ridge_weight, 0.0), row_norms


def gather_index(ids_row, rows_here, slots):
    n = ids_row.shape[1]
    owners_row = owner_of(ids_row, rows_here).astype(jnp.float32)
    same = lax.broadcasted_iota(jnp.int32, (n, n), 0) == lax.broadcasted_iota(jnp.int32, (n, n), 1)
    owners = jnp.sum(jnp.where(same, owners_row, 0.0), axis=1, keepdims=True)
    before = jnp.sum(jnp.where(owners_row < owners, 1.0, 0.0), axis=1, keepdims=True)
    position = lax.broadcasted_iota(jnp.int32, (n, 1), 0)
    return owners.astype(jnp.int32) * slots + position - before.astype(jnp.int32)


def owner_of(ids, rows_here):
    if rows_here & (rows_here - 1) == 0:
        return lax.shift_right_logical(ids, jnp.full_like(ids, rows_here.bit_length() - 1))
    return lax.div(ids, jnp.full_like(ids, rows_here))


def solve_kernel(rows_here, capacity, ids_ref, gathered_ref, emb_ref, norms_ref, change_ref, a_ref, r_ref, inv_ref):
    n, width = emb_ref.shape
    outs = change_ref.shape[0]
    slots = gathered_ref.shape[0]
    index = gather_index(ids_ref[...], rows_here, capacity)
    pick = jnp.where(lax.broadcasted_iota(jnp.int32, (n, slots), 1) == index, 1.0, 0.0).astype(jnp.bfloat16)
    block = jnp.dot(pick, gathered_ref[...], preferred_element_type=jnp.float32)
    emb = block[:, :width].astype(jnp.bfloat16)
    emb_ref[...] = emb
    res = block[:, width:width + outs] + block[:, width + outs:width + 2 * outs]
    r_ref[...] = res
    cross = lax.dot_general(emb, emb, (((1,), (1,)), ((), ())), preferred_element_type=jnp.float32)
    a, row_norms = gram_kernel(cross, width)
    norms_ref[...] = jnp.broadcast_to(row_norms, norms_ref.shape)
    a_ref[...] = a
    tiles = n // TILE
    groups = TILE // 8

    def factor(k, carry):
        here = pl.ds(pl.multiple_of(k * TILE, TILE), TILE)
        m = [a_ref[pl.ds(pl.multiple_of(k * TILE + 8 * v, 8), 8), here] for v in range(groups)]
        m = tile_inverse(m)
        for v in range(groups):
            inv_ref[k, 8 * v:8 * v + 8, :] = m[v]
        inv = inv_ref[k]
        right = a_ref[here, :]
        scaled = dot(inv, right)
        scaled_res = dot(inv, r_ref[here, :])
        rows_after = lax.broadcasted_iota(jnp.int32, (n, 1), 0) >= (k + 1) * TILE
        left = jnp.where(rows_after, a_ref[:, here], 0.0)
        a_ref[...] = a_ref[...] - dot(left, scaled)
        r_ref[...] = r_ref[...] - dot(left, scaled_res)
        return carry

    lax.fori_loop(0, tiles, factor, 0)
    for k in range(tiles - 1, -1, -1):
        lo, hi = k * TILE, (k + 1) * TILE
        rest = r_ref[lo:hi, :]
        if hi < n:
            rest = rest - dot(a_ref[lo:hi, hi:], r_ref[hi:, :])
        r_ref[lo:hi, :] = dot(inv_ref[k], rest)
    change_ref[...] = r_ref[...].T


def solve(ids, gathered, rows_here, capacity, width, outs):
    n = ids.shape[0]
    vm = pl.BlockSpec(memory_space=pltpu.VMEM)
    return pl.pallas_call(
        functools.partial(solve_kernel, rows_here, capacity),
        out_shape=(
            jax.ShapeDtypeStruct((n, width), jnp.bfloat16),
            jax.ShapeDtypeStruct((8, n), jnp.float32),
            jax.ShapeDtypeStruct((outs, n), jnp.float32),
        ),
        in_specs=[vm, vm],
        out_specs=(vm, vm, vm),
        scratch_shapes=[
            pltpu.VMEM((n, n), jnp.float32),
            pltpu.VMEM((n, outs), jnp.float32),
            pltpu.VMEM((n // TILE, TILE, TILE), jnp.float32),
        ],
        compiler_params=pltpu.CompilerParams(vmem_limit_bytes=48 * 2**20),
        name="solve",
    )(ids.reshape(1, n), gathered)


def update_kernel(base_ref, ids_ref, emb_ref, block_ref, norms_ref, change_ref, res_ref, out_ref):
    step = pl.program_id(0)
    rows, width = emb_ref.shape
    emb = emb_ref[...]
    wide = emb.astype(jnp.float32)
    row_norms = jnp.sum(wide * wide, axis=1, keepdims=True)
    cross = lax.dot_general(emb, block_ref[...], (((1,), (1,)), ((), ())), preferred_element_type=jnp.float32)
    dist = jnp.maximum(row_norms + norms_ref[0:1, :] - 2.0 * cross, 0.0)
    columns = jnp.exp(dist * (-2.0 / width))
    row = base_ref[0] + step * rows + lax.broadcasted_iota(jnp.int32, (rows, 1), 0)
    columns = columns + jnp.where(row == ids_ref[...], ridge_weight, 0.0)
    out_ref[...] = res_ref[...] - lax.dot_general(
        change_ref[...].astype(jnp.bfloat16), columns.astype(jnp.bfloat16),
        (((1,), (1,)), ((), ())), preferred_element_type=jnp.float32)


def update(base, ids, emb, block, norms, change, res_t, rows_step=512):
    rows, width = emb.shape
    n = block.shape[0]
    outs = res_t.shape[0]
    whole = lambda shape: pl.BlockSpec(shape, lambda i: (0, 0))
    return pl.pallas_call(
        update_kernel,
        grid=(rows // rows_step,),
        out_shape=jax.ShapeDtypeStruct((outs, rows), jnp.float32),
        in_specs=[
            pl.BlockSpec(memory_space=pltpu.SMEM),
            whole((1, n)),
            pl.BlockSpec((rows_step, width), lambda i: (i, 0)),
            whole((n, width)), whole((8, n)), whole((outs, n)),
            pl.BlockSpec((outs, rows_step), lambda i: (0, i)),
        ],
        out_specs=pl.BlockSpec((outs, rows_step), lambda i: (0, i)),
        compiler_params=pltpu.CompilerParams(vmem_limit_bytes=48 * 2**20),
        name="update",
    )(base, ids.reshape(1, n), emb, block, norms, change, res_t)


def pack_kernel(base_ref, ids_ref, emb_ref, res_ref, out_ref, buf_ref, sems):
    n = ids_ref.shape[0]
    outs, rows = res_ref.shape
    slots, total = out_ref.shape
    width = total - 2 * outs
    base = base_ref[0]
    first = jnp.int32(0)
    jump = 1 << (n.bit_length() - 1)
    while jump:
        ahead = first + jump
        value = ids_ref[jnp.minimum(ahead, n) - 1]
        first = jnp.where((ahead <= n) & (value < base), ahead, first)
        jump //= 2
    slot = lax.broadcasted_iota(jnp.int32, (slots, 1), 0)
    local = jnp.zeros((slots, 1), jnp.int32)
    copies = []
    for s in range(slots):
        row = jnp.clip(ids_ref[jnp.minimum(first + s, n - 1)] - base, 0, rows - 1)
        local = jnp.where(slot == s, row, local)
        group = pl.multiple_of((row >> 4) << 4, 16)
        copy = pltpu.make_async_copy(emb_ref.at[pl.ds(group, 16)], buf_ref.at[pl.ds(16 * s, 16)], sems.at[s])
        copy.start()
        copies.append(copy)
    res = res_ref[...]
    high = res.astype(jnp.bfloat16)
    low = (res - high.astype(jnp.float32)).astype(jnp.bfloat16)
    pick = jnp.where(lax.broadcasted_iota(jnp.int32, (slots, rows), 1) == local, 1.0, 0.0).astype(jnp.bfloat16)
    nt = (((1,), (1,)), ((), ()))
    high_rows = lax.dot_general(pick, high, nt, preferred_element_type=jnp.float32)
    low_rows = lax.dot_general(pick, low, nt, preferred_element_type=jnp.float32)
    out_ref[:, width:] = jnp.concatenate([high_rows, low_rows], axis=1).astype(jnp.bfloat16)
    for copy in copies:
        copy.wait()
    wanted = 16 * slot + (local & 15)
    pick = jnp.where(lax.broadcasted_iota(jnp.int32, (slots, 16 * slots), 1) == wanted, 1.0, 0.0).astype(jnp.bfloat16)
    out_ref[:, :width] = jnp.dot(pick, buf_ref[...], preferred_element_type=jnp.float32).astype(jnp.bfloat16)


def pack(base, ids, emb, res_t, slots):
    width = emb.shape[1]
    outs = res_t.shape[0]
    return pl.pallas_call(
        pack_kernel,
        out_shape=jax.ShapeDtypeStruct((slots, width + 2 * outs), jnp.bfloat16),
        in_specs=[
            pl.BlockSpec(memory_space=pltpu.SMEM), pl.BlockSpec(memory_space=pltpu.SMEM),
            pl.BlockSpec(memory_space=pl.ANY), pl.BlockSpec(memory_space=pltpu.VMEM),
        ],
        out_specs=pl.BlockSpec(memory_space=pltpu.VMEM),
        scratch_shapes=[pltpu.VMEM((16 * slots, width), jnp.bfloat16), pltpu.SemaphoreType.DMA((slots,))],
        compiler_params=pltpu.CompilerParams(vmem_limit_bytes=32 * 2**20),
        name="pack",
    )(base, ids, emb, res_t)


def gather(packed):
    return lax.all_gather(packed, ("rows", "grp"), axis=0, tiled=True)


def on_device(embeddings, residual, block_ids):
    rows_here, width = embeddings.shape
    outs = residual.shape[1]
    n = block_ids.shape[0]
    group_size = lax.axis_size("grp")
    devices = lax.axis_size("rows") * group_size
    slots = max(16, 2 * n // devices)
    base = ((lax.axis_index("rows") * group_size + lax.axis_index("grp")) * rows_here).astype(jnp.int32).reshape(1)
    res_t = residual.T
    packed = pack(base, block_ids, embeddings, res_t, slots)
    gathered = gather(packed)
    block_emb, norms, change_t = solve(block_ids, gathered, rows_here, slots, width, outs)
    updated_t = update(base, block_ids, embeddings, block_emb, norms, change_t, res_t)
    return (updated_t.T, change_t.T)


def solution(mesh):
    placed = (P(("rows", "grp"), None), P(("rows", "grp"), None), P())
    return jax.shard_map(
        on_device,
        mesh=mesh,
        in_specs=placed,
        out_specs=(P(("rows", "grp"), None), P()),
        check_vma=False,
    )
```

```python
import functools
import jax
import jax.numpy as jnp
from jax import lax
from jax.experimental import pallas as pl
from jax.experimental.pallas import tpu as pltpu
from jax.sharding import PartitionSpec as P

ridge_weight = 0.5
TILE = 128
STEP = 8
HIGH = lax.Precision.HIGHEST


def small_inverse(entries, n):
    a = {k: v for k, v in entries.items()}
    get = lambda i, j: a[(min(i, j), max(i, j))]
    for k in range(n):
        d = 1.0 / get(k, k)
        col = {i: get(i, k) for i in range(n) if i != k}
        scaled = {i: col[i] * d for i in col}
        for i in range(n):
            for j in range(i, n):
                if i != k and j != k:
                    a[(i, j)] = a[(i, j)] - scaled[i] * col[j]
        for i in col:
            a[(min(i, k), max(i, k))] = scaled[i]
        a[(k, k)] = -d
    return {k: -v for k, v in a.items()}


def tile_inverse(m):
    lane = lax.broadcasted_iota(jnp.int32, (8, TILE), 1)
    sub = lax.broadcasted_iota(jnp.int32, (8, TILE), 0)
    m = list(m)
    groups = TILE // 8
    for p in range(groups):
        c0 = p * STEP
        panel = m[p]
        entries = {
            (i, j): jnp.broadcast_to(panel[i:i + 1, c0 + j:c0 + j + 1], (8, TILE))
            for i in range(STEP) for j in range(i, STEP)
        }
        inv = small_inverse(entries, STEP)
        inside = (lane >= c0) & (lane < c0 + STEP)
        unit = jnp.where(lane - c0 == sub, 1.0, 0.0)
        augmented = jnp.where(inside, unit, panel)
        rows = [jnp.broadcast_to(augmented[j:j + 1, :], (8, TILE)) for j in range(STEP)]
        new_rows = []
        for i in range(STEP):
            acc = None
            for j in range(STEP):
                term = inv[(min(i, j), max(i, j))] * rows[j]
                acc = term if acc is None else acc + term
            new_rows.append(acc)
        for v in range(groups):
            if v == p:
                continue
            acc = jnp.where(inside, 0.0, m[v])
            for j in range(STEP):
                coef = jnp.broadcast_to(m[v][:, c0 + j:c0 + j + 1], (8, TILE))
                acc = acc - coef * new_rows[j]
            m[v] = acc
        acc = new_rows[0]
        for j in range(1, STEP):
            acc = jnp.where(sub == j, new_rows[j], acc)
        m[p] = acc
    return m


def dot(a, b, dims=((1,), (0,))):
    return lax.dot_general(a, b, (dims, ((), ())), precision=HIGH, preferred_element_type=jnp.float32)


def gram_kernel(cross, width):
    n = cross.shape[0]
    eye = (lax.broadcasted_iota(jnp.int32, (n, n), 0) == lax.broadcasted_iota(jnp.int32, (n, n), 1))
    diag = jnp.where(eye, cross, 0.0)
    row_norms = jnp.sum(diag, axis=0, keepdims=True)
    col_norms = jnp.sum(diag, axis=1, keepdims=True)
    dist = jnp.maximum(col_norms + row_norms - 2.0 * cross, 0.0)
    return jnp.exp(dist * (-2.0 / width)) + jnp.where(eye, ridge_weight, 0.0), row_norms


def gather_index(ids_row, rows_here, slots):
    n = ids_row.shape[1]
    owners_row = owner_of(ids_row, rows_here).astype(jnp.float32)
    same = lax.broadcasted_iota(jnp.int32, (n, n), 0) == lax.broadcasted_iota(jnp.int32, (n, n), 1)
    owners = jnp.sum(jnp.where(same, owners_row, 0.0), axis=1, keepdims=True)
    before = jnp.sum(jnp.where(owners_row < owners, 1.0, 0.0), axis=1, keepdims=True)
    position = lax.broadcasted_iota(jnp.int32, (n, 1), 0)
    return owners.astype(jnp.int32) * slots + position - before.astype(jnp.int32)


def owner_of(ids, rows_here):
    if rows_here & (rows_here - 1) == 0:
        return lax.shift_right_logical(ids, jnp.full_like(ids, rows_here.bit_length() - 1))
    return lax.div(ids, jnp.full_like(ids, rows_here))


def solve_kernel(rows_here, capacity, ids_ref, gathered_ref, emb_ref, norms_ref, change_ref, a_ref, r_ref, inv_ref):
    n, width = emb_ref.shape
    outs = change_ref.shape[0]
    slots = gathered_ref.shape[0]
    index = gather_index(ids_ref[...], rows_here, capacity)
    pick = jnp.where(lax.broadcasted_iota(jnp.int32, (n, slots), 1) == index, 1.0, 0.0).astype(jnp.bfloat16)
    block = jnp.dot(pick, gathered_ref[...], preferred_element_type=jnp.float32)
    emb = block[:, :width].astype(jnp.bfloat16)
    emb_ref[...] = emb
    res = block[:, width:width + outs] + block[:, width + outs:width + 2 * outs]
    r_ref[...] = res
    cross = lax.dot_general(emb, emb, (((1,), (1,)), ((), ())), preferred_element_type=jnp.float32)
    a, row_norms = gram_kernel(cross, width)
    norms_ref[...] = jnp.broadcast_to(row_norms, norms_ref.shape)
    a_ref[...] = a
    tiles = n // TILE
    groups = TILE // 8

    def factor(k, carry):
        here = pl.ds(pl.multiple_of(k * TILE, TILE), TILE)
        m = [a_ref[pl.ds(pl.multiple_of(k * TILE + 8 * v, 8), 8), here] for v in range(groups)]
        m = tile_inverse(m)
        for v in range(groups):
            inv_ref[k, 8 * v:8 * v + 8, :] = m[v]
        inv = inv_ref[k]
        right = a_ref[here, :]
        scaled = dot(inv, right)
        scaled_res = dot(inv, r_ref[here, :])
        rows_after = lax.broadcasted_iota(jnp.int32, (n, 1), 0) >= (k + 1) * TILE
        left = jnp.where(rows_after, a_ref[:, here], 0.0)
        a_ref[...] = a_ref[...] - dot(left, scaled)
        r_ref[...] = r_ref[...] - dot(left, scaled_res)
        return carry

    lax.fori_loop(0, tiles, factor, 0)
    for k in range(tiles - 1, -1, -1):
        lo, hi = k * TILE, (k + 1) * TILE
        rest = r_ref[lo:hi, :]
        if hi < n:
            rest = rest - dot(a_ref[lo:hi, hi:], r_ref[hi:, :])
        r_ref[lo:hi, :] = dot(inv_ref[k], rest)
    change_ref[...] = r_ref[...].T


def solve(ids, gathered, rows_here, capacity, width, outs):
    n = ids.shape[0]
    vm = pl.BlockSpec(memory_space=pltpu.VMEM)
    return pl.pallas_call(
        functools.partial(solve_kernel, rows_here, capacity),
        out_shape=(
            jax.ShapeDtypeStruct((n, width), jnp.bfloat16),
            jax.ShapeDtypeStruct((8, n), jnp.float32),
            jax.ShapeDtypeStruct((outs, n), jnp.float32),
        ),
        in_specs=[vm, vm],
        out_specs=(vm, vm, vm),
        scratch_shapes=[
            pltpu.VMEM((n, n), jnp.float32),
            pltpu.VMEM((n, outs), jnp.float32),
            pltpu.VMEM((n // TILE, TILE, TILE), jnp.float32),
        ],
        compiler_params=pltpu.CompilerParams(vmem_limit_bytes=48 * 2**20),
        name="solve",
    )(ids.reshape(1, n), gathered)


def update_kernel(base_ref, ids_ref, emb_ref, block_ref, norms_ref, change_ref, res_ref, out_ref):
    step = pl.program_id(0)
    rows, width = emb_ref.shape
    emb = emb_ref[...]
    wide = emb.astype(jnp.float32)
    row_norms = jnp.sum(wide * wide, axis=1, keepdims=True)
    cross = lax.dot_general(emb, block_ref[...], (((1,), (1,)), ((), ())), preferred_element_type=jnp.float32)
    dist = jnp.maximum(row_norms + norms_ref[0:1, :] - 2.0 * cross, 0.0)
    columns = jnp.exp(dist * (-2.0 / width))
    row = base_ref[0] + step * rows + lax.broadcasted_iota(jnp.int32, (rows, 1), 0)
    columns = columns + jnp.where(row == ids_ref[...], ridge_weight, 0.0)
    out_ref[...] = res_ref[...] - lax.dot_general(
        change_ref[...].astype(jnp.bfloat16), columns.astype(jnp.bfloat16),
        (((1,), (1,)), ((), ())), preferred_element_type=jnp.float32)


def update(base, ids, emb, block, norms, change, res_t, rows_step=512):
    rows, width = emb.shape
    n = block.shape[0]
    outs = res_t.shape[0]
    whole = lambda shape: pl.BlockSpec(shape, lambda i: (0, 0))
    return pl.pallas_call(
        update_kernel,
        grid=(rows // rows_step,),
        out_shape=jax.ShapeDtypeStruct((outs, rows), jnp.float32),
        in_specs=[
            pl.BlockSpec(memory_space=pltpu.SMEM),
            whole((1, n)),
            pl.BlockSpec((rows_step, width), lambda i: (i, 0)),
            whole((n, width)), whole((8, n)), whole((outs, n)),
            pl.BlockSpec((outs, rows_step), lambda i: (0, i)),
        ],
        out_specs=pl.BlockSpec((outs, rows_step), lambda i: (0, i)),
        compiler_params=pltpu.CompilerParams(vmem_limit_bytes=48 * 2**20),
        name="update",
    )(base, ids.reshape(1, n), emb, block, norms, change, res_t)


def pack_kernel(base_ref, ids_ref, emb_ref, res_ref, out_ref, buf_ref, sems):
    n = ids_ref.shape[0]
    outs, rows = res_ref.shape
    slots, total = out_ref.shape
    width = total - 2 * outs
    base = base_ref[0]
    first = jnp.int32(0)
    jump = 1 << (n.bit_length() - 1)
    while jump:
        ahead = first + jump
        value = ids_ref[jnp.minimum(ahead, n) - 1]
        first = jnp.where((ahead <= n) & (value < base), ahead, first)
        jump //= 2
    slot = lax.broadcasted_iota(jnp.int32, (slots, 1), 0)
    local = jnp.zeros((slots, 1), jnp.int32)
    copies = []
    for s in range(slots):
        row = jnp.clip(ids_ref[jnp.minimum(first + s, n - 1)] - base, 0, rows - 1)
        local = jnp.where(slot == s, row, local)
        group = pl.multiple_of((row >> 4) << 4, 16)
        copy = pltpu.make_async_copy(emb_ref.at[pl.ds(group, 16)], buf_ref.at[pl.ds(16 * s, 16)], sems.at[s])
        copy.start()
        copies.append(copy)
    res = res_ref[...]
    high = res.astype(jnp.bfloat16)
    low = (res - high.astype(jnp.float32)).astype(jnp.bfloat16)
    pick = jnp.where(lax.broadcasted_iota(jnp.int32, (slots, rows), 1) == local, 1.0, 0.0).astype(jnp.bfloat16)
    nt = (((1,), (1,)), ((), ()))
    high_rows = lax.dot_general(pick, high, nt, preferred_element_type=jnp.float32)
    low_rows = lax.dot_general(pick, low, nt, preferred_element_type=jnp.float32)
    out_ref[:, width:] = jnp.concatenate([high_rows, low_rows], axis=1).astype(jnp.bfloat16)
    for copy in copies:
        copy.wait()
    wanted = 16 * slot + (local & 15)
    pick = jnp.where(lax.broadcasted_iota(jnp.int32, (slots, 16 * slots), 1) == wanted, 1.0, 0.0).astype(jnp.bfloat16)
    out_ref[:, :width] = jnp.dot(pick, buf_ref[...], preferred_element_type=jnp.float32).astype(jnp.bfloat16)


def pack(base, ids, emb, res_t, slots):
    width = emb.shape[1]
    outs = res_t.shape[0]
    return pl.pallas_call(
        pack_kernel,
        out_shape=jax.ShapeDtypeStruct((slots, width + 2 * outs), jnp.bfloat16),
        in_specs=[
            pl.BlockSpec(memory_space=pltpu.SMEM), pl.BlockSpec(memory_space=pltpu.SMEM),
            pl.BlockSpec(memory_space=pl.ANY), pl.BlockSpec(memory_space=pltpu.VMEM),
        ],
        out_specs=pl.BlockSpec(memory_space=pltpu.VMEM),
        scratch_shapes=[pltpu.VMEM((16 * slots, width), jnp.bfloat16), pltpu.SemaphoreType.DMA((slots,))],
        compiler_params=pltpu.CompilerParams(vmem_limit_bytes=32 * 2**20),
        name="pack",
    )(base, ids, emb, res_t)


def gather_kernel(shape, packed_ref, out_ref, send_sems, recv_sems):
    n_far, n_side = shape
    slots, total = packed_ref.shape
    half = (total // 256) * 128
    r, g = lax.axis_index("rows"), lax.axis_index("grp")
    group = 2 * n_side
    z, x, y, c = r // 2, r % 2, g // 2, g % 2
    across = 1 - x
    other = 1 - c

    def place(z, x, y, c):
        return pl.ds(pl.multiple_of(((2 * z + x) * group + 2 * y + c) * slots, slots), slots)

    def device(z, x, y, c):
        return (2 * z + x, 2 * y + c)

    targets = [device((z + k) % n_far, x, y, c) for k in range(1, n_far)]
    targets += [device(z, across, y, c), device(z, x, y, other)]
    targets += [device(z, x, (y + j) % n_side, c) for j in range(1, n_side)]
    barrier = pltpu.get_barrier_semaphore()
    for target in targets:
        pl.semaphore_signal(barrier, inc=1, device_id=target, device_id_type=pl.DeviceIdType.MESH)
    pl.semaphore_wait(barrier, len(targets))
    started = []

    def send(source, region, target):
        at = len(started)
        copy = pltpu.make_async_remote_copy(
            src_ref=source, dst_ref=out_ref.at[region], send_sem=send_sems.at[at], recv_sem=recv_sems.at[at],
            device_id=target, device_id_type=pl.DeviceIdType.MESH)
        copy.start()
        started.append(copy)
        return copy

    own = place(z, x, y, c)
    full, left, right = slice(0, total), slice(0, half), slice(half, total)
    far, wide, deep, core = [], {}, {}, []
    for k in range(1, n_far):
        far.append(send(packed_ref, (own, full), device((z + k) % n_far, x, y, c)))

    def spread(k, source, where):
        wide[k] = send(source, (where, full), device(z, across, y, c))
        for j in range(1, n_side):
            deep[k, j] = send(source, (where, full), device(z, x, (y + j) % n_side, c))
        core.append(send(source, (where, full), device(z, x, y, other)))

    spread(0, packed_ref, own)
    out_ref[own, :] = packed_ref[...]
    corners = []

    def turn(k):
        from_z = (z - k + n_far) % n_far
        wide[k].wait_recv()
        here = place(from_z, across, y, c)
        for j in range(1, n_side):
            corners.append((send(out_ref.at[here, left], (here, left), device(z, x, (y + j) % n_side, c)),
                            (place(from_z, across, (y - j + n_side) % n_side, c), left)))
        core.append(send(out_ref.at[here, full], (here, full), device(z, x, y, other)))
        for j in range(1, n_side):
            deep[k, j].wait_recv()
            here = place(from_z, x, (y - j + n_side) % n_side, c)
            corners.append((send(out_ref.at[here, right], (here, right), device(z, across, y, c)),
                            (place(from_z, across, (y - j + n_side) % n_side, c), right)))
            core.append(send(out_ref.at[here, full], (here, full), device(z, x, y, other)))

    for k in range(1, n_far):
        far[k - 1].wait_recv()
        here = place((z - k + n_far) % n_far, x, y, c)
        spread(k, out_ref.at[here, full], here)
        turn(k - 1)
    turn(n_far - 1)
    for copy, region in corners:
        copy.wait_recv()
        core.append(send(out_ref.at[region], region, device(z, x, y, other)))
    for copy in core:
        copy.wait_recv()
    for copy in started:
        copy.wait_send()


def gather(packed):
    n_rows, n_grp = lax.axis_size("rows"), lax.axis_size("grp")
    n_far, n_side = n_rows // 2, n_grp // 2
    slots, total = packed.shape
    count = (n_far - 1) + n_far * (n_side + 1) + n_far * (3 * (n_side - 1) + 1)
    count += 2 * n_far * (n_side - 1) + n_far
    vm = pl.BlockSpec(memory_space=pltpu.VMEM)
    return pl.pallas_call(
        functools.partial(gather_kernel, (n_far, n_side)),
        out_shape=jax.ShapeDtypeStruct((n_rows * n_grp * slots, total), packed.dtype),
        in_specs=[vm],
        out_specs=vm,
        scratch_shapes=[pltpu.SemaphoreType.DMA((count,)), pltpu.SemaphoreType.DMA((count,))],
        compiler_params=pltpu.CompilerParams(
            collective_id=0, has_side_effects=True, vmem_limit_bytes=32 * 2**20),
        name="gather",
    )(packed)


def on_device(embeddings, residual, block_ids):
    rows_here, width = embeddings.shape
    outs = residual.shape[1]
    n = block_ids.shape[0]
    group_size = lax.axis_size("grp")
    devices = lax.axis_size("rows") * group_size
    slots = max(16, 2 * n // devices)
    base = ((lax.axis_index("rows") * group_size + lax.axis_index("grp")) * rows_here).astype(jnp.int32).reshape(1)
    res_t = residual.T
    packed = pack(base, block_ids, embeddings, res_t, slots)
    gathered = gather(packed)
    block_emb, norms, change_t = solve(block_ids, gathered, rows_here, slots, width, outs)
    updated_t = update(base, block_ids, embeddings, block_emb, norms, change_t, res_t)
    return (updated_t.T, change_t.T)


def solution(mesh):
    placed = (P(("rows", "grp"), None), P(("rows", "grp"), None), P())
    return jax.shard_map(
        on_device,
        mesh=mesh,
        in_specs=placed,
        out_specs=(P(("rows", "grp"), None), P()),
        check_vma=False,
    )
```

```python
import functools
import jax
import jax.numpy as jnp
from jax import lax
from jax.experimental import pallas as pl
from jax.experimental.pallas import tpu as pltpu
from jax.sharding import PartitionSpec as P

ridge_weight = 0.5
TILE = 128
STEP = 8
PART = 512
PANEL = 32
HIGH = lax.Precision.HIGHEST


def inverse_of(x):
    d = pl.reciprocal(x, approx=True)
    return d * (2.0 - x * d)


def small_inverse(entries, n):
    a = dict(entries)
    at = lambda i, j: (min(i, j), max(i, j))
    for k in range(0, n, 2):
        first, mixed, second = a[k, k], a[k, k + 1], a[k + 1, k + 1]
        d = inverse_of(first * second - mixed * mixed)
        p, q, r = second * d, -mixed * d, first * d
        others = [i for i in range(n) if i not in (k, k + 1)]
        one = {i: a[at(i, k)] for i in others}
        two = {i: a[at(i, k + 1)] for i in others}
        u = {i: p * one[i] + q * two[i] for i in others}
        v = {i: q * one[i] + r * two[i] for i in others}
        for i in others:
            for j in others:
                if i <= j:
                    a[i, j] = a[i, j] - (u[i] * one[j] + v[i] * two[j])
        for i in others:
            a[at(i, k)] = u[i]
            a[at(i, k + 1)] = v[i]
        a[k, k], a[k, k + 1], a[k + 1, k + 1] = -p, -q, -r
    return {k: -v for k, v in a.items()}


def tile_inverse(m):
    lane = lax.broadcasted_iota(jnp.int32, (8, TILE), 1)
    sub = lax.broadcasted_iota(jnp.int32, (8, TILE), 0)
    m = list(m)
    groups = TILE // 8
    per = PANEL // 8
    for q in range(TILE // PANEL):
        panel_groups = range(q * per, (q + 1) * per)
        for p in panel_groups:
            c0 = p * STEP
            panel = m[p]
            inside = (lane >= c0) & (lane < c0 + STEP)
            spread = [jnp.broadcast_to(panel[:, c0 + j:c0 + j + 1], (8, TILE)) for j in range(STEP)]
            entries = {
                (i, j): jnp.broadcast_to(spread[j][i:i + 1, :], (8, TILE))
                for i in range(STEP) for j in range(i, STEP)
            }
            inv = small_inverse(entries, STEP)
            augmented = jnp.where(inside, jnp.where(lane - c0 == sub, 1.0, 0.0), panel)
            rows = [jnp.broadcast_to(augmented[j:j + 1, :], (8, TILE)) for j in range(STEP)]
            new_rows = []
            for i in range(STEP):
                terms = [inv[(min(i, j), max(i, j))] * rows[j] for j in range(STEP)]
                new_rows.append(tree_sum(terms))
            for v in panel_groups:
                if v == p:
                    continue
                terms = [jnp.broadcast_to(m[v][:, c0 + j:c0 + j + 1], (8, TILE)) * new_rows[j] for j in range(STEP)]
                m[v] = jnp.where(inside, 0.0, m[v]) - tree_sum(terms)
            acc = new_rows[0]
            for j in range(1, STEP):
                acc = jnp.where(sub == j, new_rows[j], acc)
            m[p] = acc
        if per < groups:
            zero = jnp.zeros((8, TILE), jnp.float32)
            factor_rows = jnp.concatenate([m[v] if v in panel_groups else zero for v in range(groups)], axis=0)
            others = [v for v in range(groups) if v not in panel_groups]
            rest = jnp.concatenate([m[v] for v in others], axis=0)
            lanes = lax.broadcasted_iota(jnp.int32, rest.shape, 1)
            inside = (lanes >= q * PANEL) & (lanes < (q + 1) * PANEL)
            rest = jnp.where(inside, 0.0, rest) - dot(jnp.where(inside, rest, 0.0), factor_rows)
            for at, v in enumerate(others):
                m[v] = rest[8 * at:8 * at + 8]
    return m


def tree_sum(terms):
    while len(terms) > 1:
        terms = [terms[t] + terms[t + 1] for t in range(0, len(terms) - 1, 2)] + terms[len(terms) & ~1:]
    return terms[0]


def dot(a, b, dims=((1,), (0,))):
    return lax.dot_general(a, b, (dims, ((), ())), precision=HIGH, preferred_element_type=jnp.float32)


def gram_kernel(cross, width):
    n = cross.shape[0]
    eye = (lax.broadcasted_iota(jnp.int32, (n, n), 0) == lax.broadcasted_iota(jnp.int32, (n, n), 1))
    diag = jnp.where(eye, cross, 0.0)
    row_norms = jnp.sum(diag, axis=0, keepdims=True)
    col_norms = jnp.sum(diag, axis=1, keepdims=True)
    dist = jnp.maximum(col_norms + row_norms - 2.0 * cross, 0.0)
    return jnp.exp(dist * (-2.0 / width)) + jnp.where(eye, ridge_weight, 0.0), row_norms


def gather_index(ids_row, rows_here, slots):
    n = ids_row.shape[1]
    owners_row = owner_of(ids_row, rows_here).astype(jnp.float32)
    same = lax.broadcasted_iota(jnp.int32, (n, n), 0) == lax.broadcasted_iota(jnp.int32, (n, n), 1)
    owners = jnp.sum(jnp.where(same, owners_row, 0.0), axis=1, keepdims=True)
    before = jnp.sum(jnp.where(owners_row < owners, 1.0, 0.0), axis=1, keepdims=True)
    position = lax.broadcasted_iota(jnp.int32, (n, 1), 0)
    return owners.astype(jnp.int32) * slots + position - before.astype(jnp.int32)


def owner_of(ids, rows_here):
    if rows_here & (rows_here - 1) == 0:
        return lax.shift_right_logical(ids, jnp.full_like(ids, rows_here.bit_length() - 1))
    return lax.div(ids, jnp.full_like(ids, rows_here))


def solve_kernel(rows_here, capacity, ids_ref, gathered_ref, emb_ref, norms_ref, change_ref, a_ref, r_ref, inv_ref):
    n, width = emb_ref.shape
    outs = change_ref.shape[0]
    slots = gathered_ref.shape[0]
    index = gather_index(ids_ref[...], rows_here, capacity)
    pick = jnp.where(lax.broadcasted_iota(jnp.int32, (n, slots), 1) == index, 1.0, 0.0).astype(jnp.bfloat16)
    block = jnp.dot(pick, gathered_ref[...], preferred_element_type=jnp.float32)
    emb = block[:, :width].astype(jnp.bfloat16)
    emb_ref[...] = emb
    res = block[:, width:width + outs] + block[:, width + outs:width + 2 * outs]
    r_ref[...] = res
    cross = lax.dot_general(emb, emb, (((1,), (1,)), ((), ())), preferred_element_type=jnp.float32)
    a, row_norms = gram_kernel(cross, width)
    norms_ref[...] = jnp.broadcast_to(row_norms, norms_ref.shape)
    a_ref[...] = a
    tiles = n // TILE
    groups = TILE // 8

    def factor(k, carry):
        here = pl.ds(pl.multiple_of(k * TILE, TILE), TILE)
        m = [a_ref[pl.ds(pl.multiple_of(k * TILE + 8 * v, 8), 8), here] for v in range(groups)]
        m = tile_inverse(m)
        for v in range(groups):
            inv_ref[k, 8 * v:8 * v + 8, :] = m[v]
        inv = inv_ref[k]
        right = a_ref[here, :]
        scaled = dot(inv, right)
        scaled_res = dot(inv, r_ref[here, :])
        rows_after = lax.broadcasted_iota(jnp.int32, (n, 1), 0) >= (k + 1) * TILE
        left = jnp.where(rows_after, a_ref[:, here], 0.0)
        a_ref[...] = a_ref[...] - dot(left, scaled)
        r_ref[...] = r_ref[...] - dot(left, scaled_res)
        return carry

    lax.fori_loop(0, tiles, factor, 0)
    for k in range(tiles - 1, -1, -1):
        lo, hi = k * TILE, (k + 1) * TILE
        rest = r_ref[lo:hi, :]
        if hi < n:
            rest = rest - dot(a_ref[lo:hi, hi:], r_ref[hi:, :])
        r_ref[lo:hi, :] = dot(inv_ref[k], rest)
    change_ref[...] = r_ref[...].T


def solve(ids, gathered, rows_here, capacity, width, outs):
    n = ids.shape[0]
    vm = pl.BlockSpec(memory_space=pltpu.VMEM)
    return pl.pallas_call(
        functools.partial(solve_kernel, rows_here, capacity),
        out_shape=(
            jax.ShapeDtypeStruct((n, width), jnp.bfloat16),
            jax.ShapeDtypeStruct((8, n), jnp.float32),
            jax.ShapeDtypeStruct((outs, n), jnp.float32),
        ),
        in_specs=[vm, vm],
        out_specs=(vm, vm, vm),
        scratch_shapes=[
            pltpu.VMEM((n, n), jnp.float32),
            pltpu.VMEM((n, outs), jnp.float32),
            pltpu.VMEM((n // TILE, TILE, TILE), jnp.float32),
        ],
        compiler_params=pltpu.CompilerParams(vmem_limit_bytes=48 * 2**20),
        name="solve",
    )(ids.reshape(1, n), gathered)


def update_kernel(base_ref, ids_ref, emb_ref, block_ref, norms_ref, change_ref, res_ref, out_ref, block_t_ref, change_t_ref):
    step = pl.program_id(0)
    rows, width = emb_ref.shape
    rate = 2.0 / width * 1.4426950408889634

    @pl.when(step == 0)
    def _():
        block_t_ref[...] = block_ref[...].T
        change_t_ref[...] = change_ref[...].T.astype(jnp.bfloat16)

    block_norms = norms_ref[0:1, :] * rate
    ids = ids_ref[...] - (base_ref[0] + step * rows)
    part = min(rows, PART)
    for lo in range(0, rows, part):
        emb = emb_ref[lo:lo + part, :]
        wide = emb.astype(jnp.float32)
        row_norms = jnp.sum(wide * wide, axis=1, keepdims=True) * rate
        cross = jnp.dot(emb, block_t_ref[...], preferred_element_type=jnp.float32)
        columns = jnp.exp2(jnp.minimum(cross * (2.0 * rate) - (row_norms + block_norms), 0.0))
        row = lo + lax.broadcasted_iota(jnp.int32, (part, 1), 0)
        columns = jnp.where(row == ids, columns + ridge_weight, columns)
        taken = jnp.dot(columns.astype(jnp.bfloat16), change_t_ref[...], preferred_element_type=jnp.float32)
        out_ref[:, lo:lo + part] = res_ref[:, lo:lo + part] - taken.T


def update(base, ids, emb, block, norms, change, res_t, rows_step=512):
    rows, width = emb.shape
    n = block.shape[0]
    outs = res_t.shape[0]
    whole = lambda shape: pl.BlockSpec(shape, lambda i: (0, 0))
    return pl.pallas_call(
        update_kernel,
        grid=(rows // rows_step,),
        out_shape=jax.ShapeDtypeStruct((outs, rows), jnp.float32),
        in_specs=[
            pl.BlockSpec(memory_space=pltpu.SMEM),
            whole((1, n)),
            pl.BlockSpec((rows_step, width), lambda i: (i, 0)),
            whole((n, width)), whole((8, n)), whole((outs, n)),
            pl.BlockSpec((outs, rows_step), lambda i: (0, i)),
        ],
        out_specs=pl.BlockSpec((outs, rows_step), lambda i: (0, i)),
        scratch_shapes=[pltpu.VMEM((width, n), jnp.bfloat16), pltpu.VMEM((n, outs), jnp.bfloat16)],
        compiler_params=pltpu.CompilerParams(vmem_limit_bytes=60 * 2**20),
        name="update",
    )(base, ids.reshape(1, n), emb, block, norms, change, res_t)


def pack_kernel(base_ref, ids_ref, emb_ref, res_ref, out_ref, buf_ref, sems):
    n = ids_ref.shape[0]
    outs, rows = res_ref.shape
    slots, total = out_ref.shape
    width = total - 2 * outs
    base = base_ref[0]
    first = jnp.int32(0)
    jump = 1 << (n.bit_length() - 1)
    while jump:
        ahead = first + jump
        value = ids_ref[jnp.minimum(ahead, n) - 1]
        first = jnp.where((ahead <= n) & (value < base), ahead, first)
        jump //= 2
    slot = lax.broadcasted_iota(jnp.int32, (slots, 1), 0)
    local = jnp.zeros((slots, 1), jnp.int32)
    copies = []
    for s in range(slots):
        row = jnp.clip(ids_ref[jnp.minimum(first + s, n - 1)] - base, 0, rows - 1)
        local = jnp.where(slot == s, row, local)
        group = pl.multiple_of((row >> 4) << 4, 16)
        copy = pltpu.make_async_copy(emb_ref.at[pl.ds(group, 16)], buf_ref.at[pl.ds(16 * s, 16)], sems.at[s])
        copy.start()
        copies.append(copy)
    res = res_ref[...]
    high = res.astype(jnp.bfloat16)
    low = (res - high.astype(jnp.float32)).astype(jnp.bfloat16)
    pick = jnp.where(lax.broadcasted_iota(jnp.int32, (slots, rows), 1) == local, 1.0, 0.0).astype(jnp.bfloat16)
    nt = (((1,), (1,)), ((), ()))
    high_rows = lax.dot_general(pick, high, nt, preferred_element_type=jnp.float32)
    low_rows = lax.dot_general(pick, low, nt, preferred_element_type=jnp.float32)
    out_ref[:, width:] = jnp.concatenate([high_rows, low_rows], axis=1).astype(jnp.bfloat16)
    for copy in copies:
        copy.wait()
    wanted = 16 * slot + (local & 15)
    pick = jnp.where(lax.broadcasted_iota(jnp.int32, (slots, 16 * slots), 1) == wanted, 1.0, 0.0).astype(jnp.bfloat16)
    out_ref[:, :width] = jnp.dot(pick, buf_ref[...], preferred_element_type=jnp.float32).astype(jnp.bfloat16)


def pack(base, ids, emb, res_t, slots):
    width = emb.shape[1]
    outs = res_t.shape[0]
    return pl.pallas_call(
        pack_kernel,
        out_shape=jax.ShapeDtypeStruct((slots, width + 2 * outs), jnp.bfloat16),
        in_specs=[
            pl.BlockSpec(memory_space=pltpu.SMEM), pl.BlockSpec(memory_space=pltpu.SMEM),
            pl.BlockSpec(memory_space=pl.ANY), pl.BlockSpec(memory_space=pltpu.VMEM),
        ],
        out_specs=pl.BlockSpec(memory_space=pltpu.VMEM),
        scratch_shapes=[pltpu.VMEM((16 * slots, width), jnp.bfloat16), pltpu.SemaphoreType.DMA((slots,))],
        compiler_params=pltpu.CompilerParams(vmem_limit_bytes=60 * 2**20),
        name="pack",
    )(base, ids, emb, res_t)


def gather_kernel(shape, packed_ref, out_ref, send_sems, recv_sems):
    n_far, n_side = shape
    slots, total = packed_ref.shape
    half = (total // 256) * 128
    r, g = lax.axis_index("rows"), lax.axis_index("grp")
    group = 2 * n_side
    z, x, y, c = r // 2, r % 2, g // 2, g % 2
    across = 1 - x
    other = 1 - c

    def place(z, x, y, c):
        return pl.ds(pl.multiple_of(((2 * z + x) * group + 2 * y + c) * slots, slots), slots)

    def device(z, x, y, c):
        return (2 * z + x, 2 * y + c)

    targets = [device((z + k) % n_far, x, y, c) for k in range(1, n_far)]
    targets += [device(z, across, y, c), device(z, x, y, other)]
    targets += [device(z, x, (y + j) % n_side, c) for j in range(1, n_side)]
    barrier = pltpu.get_barrier_semaphore()
    for target in targets:
        pl.semaphore_signal(barrier, inc=1, device_id=target, device_id_type=pl.DeviceIdType.MESH)
    pl.semaphore_wait(barrier, len(targets))
    started = []

    def send(source, region, target):
        at = len(started)
        copy = pltpu.make_async_remote_copy(
            src_ref=source, dst_ref=out_ref.at[region], send_sem=send_sems.at[at], recv_sem=recv_sems.at[at],
            device_id=target, device_id_type=pl.DeviceIdType.MESH)
        copy.start()
        started.append(copy)
        return copy

    own = place(z, x, y, c)
    full, left, right = slice(0, total), slice(0, half), slice(half, total)
    far, wide, deep, core = [], {}, {}, []
    for k in range(1, n_far):
        far.append(send(packed_ref, (own, full), device((z + k) % n_far, x, y, c)))

    def spread(k, source, where):
        wide[k] = send(source, (where, full), device(z, across, y, c))
        for j in range(1, n_side):
            deep[k, j] = send(source, (where, full), device(z, x, (y + j) % n_side, c))
        core.append(send(source, (where, full), device(z, x, y, other)))

    spread(0, packed_ref, own)
    out_ref[own, :] = packed_ref[...]
    corners = []

    def turn(k):
        from_z = (z - k + n_far) % n_far
        wide[k].wait_recv()
        here = place(from_z, across, y, c)
        for j in range(1, n_side):
            corners.append((send(out_ref.at[here, left], (here, left), device(z, x, (y + j) % n_side, c)),
                            (place(from_z, across, (y - j + n_side) % n_side, c), left)))
        core.append(send(out_ref.at[here, full], (here, full), device(z, x, y, other)))
        for j in range(1, n_side):
            deep[k, j].wait_recv()
            here = place(from_z, x, (y - j + n_side) % n_side, c)
            corners.append((send(out_ref.at[here, right], (here, right), device(z, across, y, c)),
                            (place(from_z, across, (y - j + n_side) % n_side, c), right)))
            core.append(send(out_ref.at[here, full], (here, full), device(z, x, y, other)))

    for k in range(1, n_far):
        far[k - 1].wait_recv()
        here = place((z - k + n_far) % n_far, x, y, c)
        spread(k, out_ref.at[here, full], here)
        turn(k - 1)
    turn(n_far - 1)
    for copy, region in corners:
        copy.wait_recv()
        core.append(send(out_ref.at[region], region, device(z, x, y, other)))
    for copy in core:
        copy.wait_recv()
    for copy in started:
        copy.wait_send()


def gather(packed):
    n_rows, n_grp = lax.axis_size("rows"), lax.axis_size("grp")
    n_far, n_side = n_rows // 2, n_grp // 2
    slots, total = packed.shape
    count = (n_far - 1) + n_far * (n_side + 1) + n_far * (3 * (n_side - 1) + 1)
    count += 2 * n_far * (n_side - 1) + n_far
    vm = pl.BlockSpec(memory_space=pltpu.VMEM)
    return pl.pallas_call(
        functools.partial(gather_kernel, (n_far, n_side)),
        out_shape=jax.ShapeDtypeStruct((n_rows * n_grp * slots, total), packed.dtype),
        in_specs=[vm],
        out_specs=vm,
        scratch_shapes=[pltpu.SemaphoreType.DMA((count,)), pltpu.SemaphoreType.DMA((count,))],
        compiler_params=pltpu.CompilerParams(
            collective_id=0, has_side_effects=True, vmem_limit_bytes=32 * 2**20),
        name="gather",
    )(packed)


def on_device(embeddings, residual, block_ids):
    rows_here, width = embeddings.shape
    outs = residual.shape[1]
    n = block_ids.shape[0]
    group_size = lax.axis_size("grp")
    devices = lax.axis_size("rows") * group_size
    slots = max(16, 2 * n // devices)
    base = ((lax.axis_index("rows") * group_size + lax.axis_index("grp")) * rows_here).astype(jnp.int32).reshape(1)
    res_t = residual.T
    packed = pack(base, block_ids, embeddings, res_t, slots)
    gathered = gather(packed)
    block_emb, norms, change_t = solve(block_ids, gathered, rows_here, slots, width, outs)
    updated_t = update(base, block_ids, embeddings, block_emb, norms, change_t, res_t)
    return (updated_t.T, change_t.T)


def solution(mesh):
    placed = (P(("rows", "grp"), None), P(("rows", "grp"), None), P())
    return jax.shard_map(
        on_device,
        mesh=mesh,
        in_specs=placed,
        out_specs=(P(("rows", "grp"), None), P()),
        check_vma=False,
    )
```

```python
import functools
import jax
import jax.numpy as jnp
from jax import lax
from jax.experimental import pallas as pl
from jax.experimental.pallas import tpu as pltpu
from jax.sharding import PartitionSpec as P

ridge_weight = 0.5
TILE = 128
STEP = 8
PART = 512
PANEL = 32
HIGH = lax.Precision.HIGHEST


def inverse_of(x):
    d = pl.reciprocal(x, approx=True)
    return d * (2.0 - x * d)


def small_inverse(entries, n):
    a = dict(entries)
    at = lambda i, j: (min(i, j), max(i, j))
    for k in range(0, n, 2):
        first, mixed, second = a[k, k], a[k, k + 1], a[k + 1, k + 1]
        d = inverse_of(first * second - mixed * mixed)
        p, q, r = second * d, -mixed * d, first * d
        others = [i for i in range(n) if i not in (k, k + 1)]
        one = {i: a[at(i, k)] for i in others}
        two = {i: a[at(i, k + 1)] for i in others}
        u = {i: p * one[i] + q * two[i] for i in others}
        v = {i: q * one[i] + r * two[i] for i in others}
        for i in others:
            for j in others:
                if i <= j:
                    a[i, j] = a[i, j] - (u[i] * one[j] + v[i] * two[j])
        for i in others:
            a[at(i, k)] = u[i]
            a[at(i, k + 1)] = v[i]
        a[k, k], a[k, k + 1], a[k + 1, k + 1] = -p, -q, -r
    return {k: -v for k, v in a.items()}


def tile_inverse(m):
    lane = lax.broadcasted_iota(jnp.int32, (8, TILE), 1)
    sub = lax.broadcasted_iota(jnp.int32, (8, TILE), 0)
    m = list(m)
    groups = TILE // 8
    per = PANEL // 8
    for q in range(TILE // PANEL):
        panel_groups = range(q * per, (q + 1) * per)
        for p in panel_groups:
            c0 = p * STEP
            panel = m[p]
            inside = (lane >= c0) & (lane < c0 + STEP)
            spread = [jnp.broadcast_to(panel[:, c0 + j:c0 + j + 1], (8, TILE)) for j in range(STEP)]
            entries = {
                (i, j): jnp.broadcast_to(spread[j][i:i + 1, :], (8, TILE))
                for i in range(STEP) for j in range(i, STEP)
            }
            inv = small_inverse(entries, STEP)
            augmented = jnp.where(inside, jnp.where(lane - c0 == sub, 1.0, 0.0), panel)
            rows = [jnp.broadcast_to(augmented[j:j + 1, :], (8, TILE)) for j in range(STEP)]
            new_rows = []
            for i in range(STEP):
                terms = [inv[(min(i, j), max(i, j))] * rows[j] for j in range(STEP)]
                new_rows.append(tree_sum(terms))
            for v in panel_groups:
                if v == p:
                    continue
                terms = [jnp.broadcast_to(m[v][:, c0 + j:c0 + j + 1], (8, TILE)) * new_rows[j] for j in range(STEP)]
                m[v] = jnp.where(inside, 0.0, m[v]) - tree_sum(terms)
            acc = new_rows[0]
            for j in range(1, STEP):
                acc = jnp.where(sub == j, new_rows[j], acc)
            m[p] = acc
        if per < groups:
            zero = jnp.zeros((8, TILE), jnp.float32)
            factor_rows = jnp.concatenate([m[v] if v in panel_groups else zero for v in range(groups)], axis=0)
            others = [v for v in range(groups) if v not in panel_groups]
            rest = jnp.concatenate([m[v] for v in others], axis=0)
            lanes = lax.broadcasted_iota(jnp.int32, rest.shape, 1)
            inside = (lanes >= q * PANEL) & (lanes < (q + 1) * PANEL)
            rest = jnp.where(inside, 0.0, rest) - dot(jnp.where(inside, rest, 0.0), factor_rows)
            for at, v in enumerate(others):
                m[v] = rest[8 * at:8 * at + 8]
    return m


def tree_sum(terms):
    while len(terms) > 1:
        terms = [terms[t] + terms[t + 1] for t in range(0, len(terms) - 1, 2)] + terms[len(terms) & ~1:]
    return terms[0]


def dot(a, b, dims=((1,), (0,))):
    return lax.dot_general(a, b, (dims, ((), ())), precision=HIGH, preferred_element_type=jnp.float32)


def gram_kernel(cross, width):
    n = cross.shape[0]
    eye = (lax.broadcasted_iota(jnp.int32, (n, n), 0) == lax.broadcasted_iota(jnp.int32, (n, n), 1))
    diag = jnp.where(eye, cross, 0.0)
    row_norms = jnp.sum(diag, axis=0, keepdims=True)
    col_norms = jnp.sum(diag, axis=1, keepdims=True)
    dist = jnp.maximum(col_norms + row_norms - 2.0 * cross, 0.0)
    return jnp.exp(dist * (-2.0 / width)) + jnp.where(eye, ridge_weight, 0.0), row_norms


def gather_index(ids_row, rows_here, slots):
    n = ids_row.shape[1]
    owners_row = owner_of(ids_row, rows_here).astype(jnp.float32)
    same = lax.broadcasted_iota(jnp.int32, (n, n), 0) == lax.broadcasted_iota(jnp.int32, (n, n), 1)
    owners = jnp.sum(jnp.where(same, owners_row, 0.0), axis=1, keepdims=True)
    before = jnp.sum(jnp.where(owners_row < owners, 1.0, 0.0), axis=1, keepdims=True)
    position = lax.broadcasted_iota(jnp.int32, (n, 1), 0)
    return owners.astype(jnp.int32) * slots + position - before.astype(jnp.int32)


def owner_of(ids, rows_here):
    if rows_here & (rows_here - 1) == 0:
        return lax.shift_right_logical(ids, jnp.full_like(ids, rows_here.bit_length() - 1))
    return lax.div(ids, jnp.full_like(ids, rows_here))


def solve_kernel(rows_here, capacity, ids_ref, gathered_ref, emb_ref, norms_ref, change_ref, a_ref, r_ref, inv_ref):
    n, width = emb_ref.shape
    outs = change_ref.shape[0]
    slots = gathered_ref.shape[0]
    index = gather_index(ids_ref[...], rows_here, capacity)
    pick = jnp.where(lax.broadcasted_iota(jnp.int32, (n, slots), 1) == index, 1.0, 0.0).astype(jnp.bfloat16)
    block = jnp.dot(pick, gathered_ref[...], preferred_element_type=jnp.float32)
    emb = block[:, :width].astype(jnp.bfloat16)
    emb_ref[...] = emb
    res = block[:, width:width + outs] + block[:, width + outs:width + 2 * outs]
    r_ref[...] = res
    cross = lax.dot_general(emb, emb, (((1,), (1,)), ((), ())), preferred_element_type=jnp.float32)
    a, row_norms = gram_kernel(cross, width)
    norms_ref[...] = jnp.broadcast_to(row_norms, norms_ref.shape)
    a_ref[...] = a
    tiles = n // TILE
    groups = TILE // 8

    for k in range(tiles):
        lo, hi = k * TILE, (k + 1) * TILE
        m = tile_inverse([a_ref[lo + 8 * v:lo + 8 * v + 8, lo:hi] for v in range(groups)])
        for v in range(groups):
            inv_ref[k, 8 * v:8 * v + 8, :] = m[v]
        if hi < n:
            inv = inv_ref[k]
            left = a_ref[hi:, lo:hi]
            scaled = dot(inv, a_ref[lo:hi, hi:])
            scaled_res = dot(inv, r_ref[lo:hi, :])
            a_ref[hi:, hi:] = a_ref[hi:, hi:] - dot(left, scaled)
            r_ref[hi:, :] = r_ref[hi:, :] - dot(left, scaled_res)

    for k in range(tiles - 1, -1, -1):
        lo, hi = k * TILE, (k + 1) * TILE
        rest = r_ref[lo:hi, :]
        if hi < n:
            rest = rest - dot(a_ref[lo:hi, hi:], r_ref[hi:, :])
        r_ref[lo:hi, :] = dot(inv_ref[k], rest)
    change_ref[...] = r_ref[...].T


def solve(ids, gathered, rows_here, capacity, width, outs):
    n = ids.shape[0]
    vm = pl.BlockSpec(memory_space=pltpu.VMEM)
    return pl.pallas_call(
        functools.partial(solve_kernel, rows_here, capacity),
        out_shape=(
            jax.ShapeDtypeStruct((n, width), jnp.bfloat16),
            jax.ShapeDtypeStruct((8, n), jnp.float32),
            jax.ShapeDtypeStruct((outs, n), jnp.float32),
        ),
        in_specs=[vm, vm],
        out_specs=(vm, vm, vm),
        scratch_shapes=[
            pltpu.VMEM((n, n), jnp.float32),
            pltpu.VMEM((n, outs), jnp.float32),
            pltpu.VMEM((n // TILE, TILE, TILE), jnp.float32),
        ],
        compiler_params=pltpu.CompilerParams(vmem_limit_bytes=48 * 2**20),
        name="solve",
    )(ids.reshape(1, n), gathered)


def update_kernel(base_ref, ids_ref, emb_ref, block_ref, norms_ref, change_ref, res_ref, out_ref, block_t_ref, change_t_ref):
    step = pl.program_id(0)
    rows, width = emb_ref.shape
    rate = 2.0 / width * 1.4426950408889634

    @pl.when(step == 0)
    def _():
        block_t_ref[...] = block_ref[...].T
        change_t_ref[...] = change_ref[...].T.astype(jnp.bfloat16)

    block_norms = norms_ref[0:1, :] * rate
    ids = ids_ref[...] - (base_ref[0] + step * rows)
    part = min(rows, PART)
    for lo in range(0, rows, part):
        emb = emb_ref[lo:lo + part, :]
        wide = emb.astype(jnp.float32)
        row_norms = jnp.sum(wide * wide, axis=1, keepdims=True) * rate
        cross = jnp.dot(emb, block_t_ref[...], preferred_element_type=jnp.float32)
        columns = jnp.exp2(jnp.minimum(cross * (2.0 * rate) - (row_norms + block_norms), 0.0))
        row = lo + lax.broadcasted_iota(jnp.int32, (part, 1), 0)
        columns = jnp.where(row == ids, columns + ridge_weight, columns)
        taken = jnp.dot(columns.astype(jnp.bfloat16), change_t_ref[...], preferred_element_type=jnp.float32)
        out_ref[:, lo:lo + part] = res_ref[:, lo:lo + part] - taken.T


def update(base, ids, emb, block, norms, change, res_t, rows_step=512):
    rows, width = emb.shape
    n = block.shape[0]
    outs = res_t.shape[0]
    whole = lambda shape: pl.BlockSpec(shape, lambda i: (0, 0))
    return pl.pallas_call(
        update_kernel,
        grid=(rows // rows_step,),
        out_shape=jax.ShapeDtypeStruct((outs, rows), jnp.float32),
        in_specs=[
            pl.BlockSpec(memory_space=pltpu.SMEM),
            whole((1, n)),
            pl.BlockSpec((rows_step, width), lambda i: (i, 0)),
            whole((n, width)), whole((8, n)), whole((outs, n)),
            pl.BlockSpec((outs, rows_step), lambda i: (0, i)),
        ],
        out_specs=pl.BlockSpec((outs, rows_step), lambda i: (0, i)),
        scratch_shapes=[pltpu.VMEM((width, n), jnp.bfloat16), pltpu.VMEM((n, outs), jnp.bfloat16)],
        compiler_params=pltpu.CompilerParams(vmem_limit_bytes=60 * 2**20),
        name="update",
    )(base, ids.reshape(1, n), emb, block, norms, change, res_t)


def pack_kernel(base_ref, ids_ref, emb_ref, res_ref, out_ref, buf_ref, sems):
    n = ids_ref.shape[0]
    outs, rows = res_ref.shape
    slots, total = out_ref.shape
    width = total - 2 * outs
    base = base_ref[0]
    first = jnp.int32(0)
    jump = 1 << (n.bit_length() - 1)
    while jump:
        ahead = first + jump
        value = ids_ref[jnp.minimum(ahead, n) - 1]
        first = jnp.where((ahead <= n) & (value < base), ahead, first)
        jump //= 2
    slot = lax.broadcasted_iota(jnp.int32, (slots, 1), 0)
    local = jnp.zeros((slots, 1), jnp.int32)
    copies = []
    for s in range(slots):
        row = jnp.clip(ids_ref[jnp.minimum(first + s, n - 1)] - base, 0, rows - 1)
        local = jnp.where(slot == s, row, local)
        group = pl.multiple_of((row >> 4) << 4, 16)
        copy = pltpu.make_async_copy(emb_ref.at[pl.ds(group, 16)], buf_ref.at[pl.ds(16 * s, 16)], sems.at[s])
        copy.start()
        copies.append(copy)
    res = res_ref[...]
    high = res.astype(jnp.bfloat16)
    low = (res - high.astype(jnp.float32)).astype(jnp.bfloat16)
    pick = jnp.where(lax.broadcasted_iota(jnp.int32, (slots, rows), 1) == local, 1.0, 0.0).astype(jnp.bfloat16)
    nt = (((1,), (1,)), ((), ()))
    high_rows = lax.dot_general(pick, high, nt, preferred_element_type=jnp.float32)
    low_rows = lax.dot_general(pick, low, nt, preferred_element_type=jnp.float32)
    out_ref[:, width:] = jnp.concatenate([high_rows, low_rows], axis=1).astype(jnp.bfloat16)
    for copy in copies:
        copy.wait()
    wanted = 16 * slot + (local & 15)
    pick = jnp.where(lax.broadcasted_iota(jnp.int32, (slots, 16 * slots), 1) == wanted, 1.0, 0.0).astype(jnp.bfloat16)
    out_ref[:, :width] = jnp.dot(pick, buf_ref[...], preferred_element_type=jnp.float32).astype(jnp.bfloat16)


def pack(base, ids, emb, res_t, slots):
    width = emb.shape[1]
    outs = res_t.shape[0]
    return pl.pallas_call(
        pack_kernel,
        out_shape=jax.ShapeDtypeStruct((slots, width + 2 * outs), jnp.bfloat16),
        in_specs=[
            pl.BlockSpec(memory_space=pltpu.SMEM), pl.BlockSpec(memory_space=pltpu.SMEM),
            pl.BlockSpec(memory_space=pl.ANY), pl.BlockSpec(memory_space=pltpu.VMEM),
        ],
        out_specs=pl.BlockSpec(memory_space=pltpu.VMEM),
        scratch_shapes=[pltpu.VMEM((16 * slots, width), jnp.bfloat16), pltpu.SemaphoreType.DMA((slots,))],
        compiler_params=pltpu.CompilerParams(vmem_limit_bytes=60 * 2**20),
        name="pack",
    )(base, ids, emb, res_t)


def gather_kernel(shape, packed_ref, out_ref, send_sems, recv_sems):
    n_far, n_side = shape
    slots, total = packed_ref.shape
    half = (total // 256) * 128
    r, g = lax.axis_index("rows"), lax.axis_index("grp")
    group = 2 * n_side
    z, x, y, c = r // 2, r % 2, g // 2, g % 2
    across = 1 - x
    other = 1 - c

    def place(z, x, y, c):
        return pl.ds(pl.multiple_of(((2 * z + x) * group + 2 * y + c) * slots, slots), slots)

    def device(z, x, y, c):
        return (2 * z + x, 2 * y + c)

    targets = [device((z + k) % n_far, x, y, c) for k in range(1, n_far)]
    targets += [device(z, across, y, c), device(z, x, y, other)]
    targets += [device(z, x, (y + j) % n_side, c) for j in range(1, n_side)]
    barrier = pltpu.get_barrier_semaphore()
    for target in targets:
        pl.semaphore_signal(barrier, inc=1, device_id=target, device_id_type=pl.DeviceIdType.MESH)
    pl.semaphore_wait(barrier, len(targets))
    started = []

    def send(source, region, target):
        at = len(started)
        copy = pltpu.make_async_remote_copy(
            src_ref=source, dst_ref=out_ref.at[region], send_sem=send_sems.at[at], recv_sem=recv_sems.at[at],
            device_id=target, device_id_type=pl.DeviceIdType.MESH)
        copy.start()
        started.append(copy)
        return copy

    own = place(z, x, y, c)
    full, left, right = slice(0, total), slice(0, half), slice(half, total)
    far, wide, deep, core = [], {}, {}, []
    for k in range(1, n_far):
        far.append(send(packed_ref, (own, full), device((z + k) % n_far, x, y, c)))

    def spread(k, source, where):
        wide[k] = send(source, (where, full), device(z, across, y, c))
        for j in range(1, n_side):
            deep[k, j] = send(source, (where, full), device(z, x, (y + j) % n_side, c))
        core.append(send(source, (where, full), device(z, x, y, other)))

    spread(0, packed_ref, own)
    out_ref[own, :] = packed_ref[...]
    corners = []

    def turn(k):
        from_z = (z - k + n_far) % n_far
        wide[k].wait_recv()
        here = place(from_z, across, y, c)
        for j in range(1, n_side):
            corners.append((send(out_ref.at[here, left], (here, left), device(z, x, (y + j) % n_side, c)),
                            (place(from_z, across, (y - j + n_side) % n_side, c), left)))
        core.append(send(out_ref.at[here, full], (here, full), device(z, x, y, other)))
        for j in range(1, n_side):
            deep[k, j].wait_recv()
            here = place(from_z, x, (y - j + n_side) % n_side, c)
            corners.append((send(out_ref.at[here, right], (here, right), device(z, across, y, c)),
                            (place(from_z, across, (y - j + n_side) % n_side, c), right)))
            core.append(send(out_ref.at[here, full], (here, full), device(z, x, y, other)))

    for k in range(1, n_far):
        far[k - 1].wait_recv()
        here = place((z - k + n_far) % n_far, x, y, c)
        spread(k, out_ref.at[here, full], here)
        turn(k - 1)
    turn(n_far - 1)
    for copy, region in corners:
        copy.wait_recv()
        core.append(send(out_ref.at[region], region, device(z, x, y, other)))
    for copy in core:
        copy.wait_recv()
    for copy in started:
        copy.wait_send()


def gather(packed):
    n_rows, n_grp = lax.axis_size("rows"), lax.axis_size("grp")
    n_far, n_side = n_rows // 2, n_grp // 2
    slots, total = packed.shape
    count = (n_far - 1) + n_far * (n_side + 1) + n_far * (3 * (n_side - 1) + 1)
    count += 2 * n_far * (n_side - 1) + n_far
    vm = pl.BlockSpec(memory_space=pltpu.VMEM)
    return pl.pallas_call(
        functools.partial(gather_kernel, (n_far, n_side)),
        out_shape=jax.ShapeDtypeStruct((n_rows * n_grp * slots, total), packed.dtype),
        in_specs=[vm],
        out_specs=vm,
        scratch_shapes=[pltpu.SemaphoreType.DMA((count,)), pltpu.SemaphoreType.DMA((count,))],
        compiler_params=pltpu.CompilerParams(
            collective_id=0, has_side_effects=True, vmem_limit_bytes=32 * 2**20),
        name="gather",
    )(packed)


def on_device(embeddings, residual, block_ids):
    rows_here, width = embeddings.shape
    outs = residual.shape[1]
    n = block_ids.shape[0]
    group_size = lax.axis_size("grp")
    devices = lax.axis_size("rows") * group_size
    slots = max(16, 2 * n // devices)
    base = ((lax.axis_index("rows") * group_size + lax.axis_index("grp")) * rows_here).astype(jnp.int32).reshape(1)
    res_t = residual.T
    packed = pack(base, block_ids, embeddings, res_t, slots)
    gathered = gather(packed)
    block_emb, norms, change_t = solve(block_ids, gathered, rows_here, slots, width, outs)
    updated_t = update(base, block_ids, embeddings, block_emb, norms, change_t, res_t)
    return (updated_t.T, change_t.T)


def solution(mesh):
    placed = (P(("rows", "grp"), None), P(("rows", "grp"), None), P())
    return jax.shard_map(
        on_device,
        mesh=mesh,
        in_specs=placed,
        out_specs=(P(("rows", "grp"), None), P()),
        check_vma=False,
    )
```
